32 devices in a mesh: ep: 8 (over z, x), blk: 4 (over y, core).
Axes of the slice: x: 2, y: 2, z: 4, core: 2. Of those that a mesh axis runs over, the one named last changes fastest.
Arguments:
- tokens: bfloat16 [4096, 1536], P(('ep', 'blk')), may hold values from -6 to 6
- norm_gain: bfloat16 [1536], replicated, may hold values from 0.099609375 to 1.8984375
- router_weight: bfloat16 [1536, 8], replicated, may hold values from -0.15625 to 0.15625
- routes: int32 [4096, 4], P(('ep', 'blk')), may hold values from 0 to 7, all different within a row; in each aligned block of 128 rows (0 to 127, 128 to 255, ...) at most 96 rows name the same one
- placement: int32 [8], replicated, may hold values from 0 to 7, each once
- gate_weight: bfloat16 [8, 1536, 768], P('ep', 'blk'), may hold values from -0.15625 to 0.15625
- up_weight: bfloat16 [8, 1536, 768], P('ep', 'blk'), may hold values from -0.15625 to 0.15625
- down_weight: bfloat16 [8, 768, 1536], P('ep', 'blk'), may hold values from -0.21875 to 0.21875
Outputs:
- mixed: bfloat16 [4096, 1536], P(('ep', 'blk'))
The draws below stay inside these ranges and needn't reach their ends.
Inputs may be any that keep to these rules, and one draw needn't show every extreme that they name: `routes`: among the rows of one device, each expert is named by at most 96 rows, a bound that some block reaches; a row names 4 different experts. `placement`: each index of ep holds exactly one expert.
All inputs are finite; a program needn't handle non-finite values.
Results may differ from the reference program's by a relative error of at most 0.0071.
Values may be sent and summed in bfloat16 or wider, within the bound.
No kernel may reach another device: no remote copies, remote signals or barrier semaphores. Data moves between devices by JAX's collectives and lax.ppermute only.
A program may use at most 64 MiB of HBM per device.

```python
import math
import jax
import jax.numpy as jnp
import numpy as np
from jax import lax

D = 1536
FF = 768
TOPK = 4
TOK_DEV = 128
EXPERTS = 8
CAP = 96
TOKENS = 4096


def level_of(own_key, shape, shards, smallest, top_value):
    def one(axis_at, shards_of):
        heights = jax.random.uniform(jax.random.fold_in(jax.random.fold_in(own_key, 6), axis_at), (shards_of,), jnp.float32, smallest / len(shards), top_value / len(shards))
        return jnp.repeat(jnp.exp(heights), shape[axis_at] // shards_of).reshape((-1,) + (1,) * (len(shape) - axis_at - 1))

    loudness = one(*shards[0])
    for cut in shards[1:]:
        loudness = loudness * one(*cut)
    return loudness


def assign_block(own_key, own, number, rows, number_of, top, most, slope):
    ranking = jax.random.permutation(own_key, number_of)
    heavy_load, ordinary = shares(number_of, rows * top, most, slope, True), shares(number_of, rows * top, most, slope, False)
    places = jnp.arange(number_of)

    def named(sizes, rotation):
        used = int((sizes > 0).sum())
        fixed = max(1, used // 4)
        moved = fixed + (places - fixed + rotation * (used - fixed)) % max(1, number_of - fixed)
        return jnp.zeros((number_of,), jnp.int32).at[ranking[jnp.where(places < fixed, places, moved)]].set(jnp.asarray(sizes, jnp.int32))

    sizes = jnp.where(number % 4 == 0, named(heavy_load, number // 4), named(ordinary, number - number // 4 - 1))
    mixed = jax.random.permutation(jax.random.fold_in(own, 3), number_of)
    giver, receiver = mixed[0:number_of // 2 * 2:2], mixed[1:number_of // 2 * 2:2]
    slack = jnp.minimum(sizes[giver] - 1, most - sizes[receiver]) // 2
    slack = jnp.where((giver == ranking[0]) | (receiver == ranking[0]) | (sizes[receiver] == 0), 0, jnp.maximum(slack, 0))
    moved = jax.random.randint(jax.random.fold_in(own, 4), (number_of // 2,), 0, 1 << 20) % (slack + 1)
    sizes = sizes.at[giver].add(-moved).at[receiver].add(moved)
    items = jnp.searchsorted(jnp.cumsum(sizes), jnp.arange(rows * top), side="right").astype(jnp.int32)
    table = items.reshape(top, rows).T
    table = table[jax.random.permutation(jax.random.fold_in(own, 1), rows)]
    rotation = jax.random.randint(jax.random.fold_in(own, 2), (rows, 1), 0, top)
    return jnp.take_along_axis(table, (jnp.arange(top)[None, :] + rotation) % top, axis=1)


def shares(amount, total, bound, slope, full):
    portions = [(1 << 20) // math.isqrt(standing ** slope) + 1 for standing in range(1, amount + 1)]
    largest = bound if full else min(bound, max(-(-total // amount), total * portions[0] // sum(portions)))
    least = 1 if total - largest >= amount - 1 else 0
    holding, spare = [largest] + [least] * (amount - 1), total - largest - least * (amount - 1)
    while spare > 0:
        candidates = [i for i in range(1, amount) if holding[i] < largest] or [i for i in range(1, amount) if holding[i] < bound]
        pool, remaining = sum([portions[i] for i in candidates]), spare
        for i in candidates:
            more = min(bound - holding[i], max(1, remaining * portions[i] // pool), spare)
            holding[i] = holding[i] + more
            spare = spare - more
    return np.array(holding)


def gaussian(rng, dims, spread, most, cuts=(), kind=jnp.bfloat16):
    gain = level_of(rng, dims, cuts, -0.22, 0.18) if cuts else 1.0
    array = jax.random.normal(rng, dims, jnp.float32) * spread * gain
    return jnp.minimum(jnp.maximum(array, -most), most).astype(kind)


def setup_inputs(seed: int = 0) -> dict:
    streams_of = jax.random.split(jax.random.key(seed), 9)
    tokens = gaussian(streams_of[0], (TOKENS, D), 1.0, 6.0, ((0, 32),))
    norm_gain = jnp.clip(1.0 + 0.18 * jax.random.normal(streams_of[1], (D,), jnp.float32), 0.099609375, 1.8984375).astype(jnp.bfloat16)
    router_weight = gaussian(streams_of[2], (D, EXPERTS), D ** -0.5, 0.15625)
    routes_keys = jax.random.split(jax.random.fold_in(streams_of[3], 1), TOKENS // TOK_DEV)
    routes_turns = jax.random.permutation(jax.random.fold_in(streams_of[3], 3), TOKENS // TOK_DEV)
    routes = jax.vmap(lambda own, number: assign_block(jax.random.fold_in(streams_of[3], 2), own, number, TOK_DEV, EXPERTS, TOPK, CAP, 2))(routes_keys, routes_turns).reshape((TOKENS, TOPK))
    placement = jax.random.permutation(streams_of[4], EXPERTS).astype(jnp.int32)
    gate_weight = gaussian(streams_of[5], (EXPERTS, D, FF), D ** -0.5, 0.15625, ((0, 8), (1, 4)))
    up_weight = gaussian(streams_of[6], (EXPERTS, D, FF), D ** -0.5, 0.15625, ((0, 8), (1, 4)))
    down_weight = gaussian(streams_of[7], (EXPERTS, FF, D), FF ** -0.5, 0.21875, ((0, 8), (1, 4)))
    return {"tokens": tokens, "norm_gain": norm_gain, "router_weight": router_weight, "routes": routes, "placement": placement, "gate_weight": gate_weight, "up_weight": up_weight, "down_weight": down_weight}


def reference(tokens, norm_gain, router_weight, routes, placement, gate_weight, up_weight, down_weight):
    values = tokens.astype(jnp.float32)
    square = lax.optimization_barrier(jnp.mean(values * values, axis=-1, keepdims=True))
    normed = (values * lax.rsqrt(square + 1e-06) * norm_gain.astype(jnp.float32)).astype(jnp.bfloat16)
    logits = jnp.dot(normed, router_weight, preferred_element_type=jnp.float32)
    picked = jax.nn.sigmoid(jnp.take_along_axis(logits, routes, axis=1))
    gates = picked / lax.optimization_barrier(jnp.sum(picked, axis=1, keepdims=True))
    blocks = TOKENS // TOK_DEV
    assigned = TOK_DEV * TOPK
    flat_ids = routes.reshape(blocks, assigned)
    onehot = (flat_ids[:, :, None] == jnp.arange(EXPERTS, dtype=jnp.int32)[None, None, :]).astype(jnp.int32)
    counts = jnp.cumsum(onehot, axis=1)
    slots = lax.optimization_barrier(jnp.sum(onehot * (counts - 1), axis=-1)).astype(jnp.int32)
    targets = (jnp.arange(blocks, dtype=jnp.int32)[:, None] * CAP + slots).reshape(-1)
    flat_ids = flat_ids.reshape(-1)
    flat_gates = gates.reshape(-1)
    total = blocks * CAP
    everyone = jnp.arange(TOKENS * TOPK, dtype=jnp.int32)

    def expert_step(acc, expert):
        match = flat_ids == expert
        where_to = jnp.where(match, targets, total).astype(jnp.int32)
        owner = jnp.full((total,), -1, jnp.int32).at[where_to].set(everyone, mode='drop')
        valid = owner >= 0
        owned = jnp.maximum(owner, 0)
        token_rows = owned // TOPK
        buffer = jnp.where(valid[:, None], normed[token_rows], jnp.zeros((), jnp.bfloat16))
        holder = placement[expert]
        gate = jnp.dot(buffer, gate_weight[holder], preferred_element_type=jnp.float32)
        upper = jnp.dot(buffer, up_weight[holder], preferred_element_type=jnp.float32)
        hidden = (jax.nn.relu(gate) * upper).astype(jnp.bfloat16)
        rows_out = jnp.dot(hidden, down_weight[holder], preferred_element_type=jnp.float32).astype(jnp.bfloat16)
        weights = jnp.where(valid, flat_gates[owned], jnp.zeros((), jnp.float32))
        acc = acc.at[token_rows].add(weights[:, None] * rows_out.astype(jnp.float32))
        return (acc, None)
    start = jnp.zeros((TOKENS, D), jnp.float32)
    acc, unused = lax.scan(expert_step, start, jnp.arange(EXPERTS, dtype=jnp.int32))
    return acc.astype(jnp.bfloat16)
```

```python
import functools

import jax
import jax.numpy as jnp
from jax import lax
from jax.experimental import pallas as pl
from jax.experimental.pallas import tpu as pltpu
from jax.sharding import PartitionSpec as P

VMEM_LIMIT = 28 * 1024 * 1024
WHOLE = pl.BlockSpec(memory_space=pltpu.VMEM)
SCALAR = pl.BlockSpec(memory_space=pltpu.SMEM)
ANYWHERE = pl.BlockSpec(memory_space=pl.ANY)


def params():
    return pltpu.CompilerParams(vmem_limit_bytes=VMEM_LIMIT)


def cost(flops, moved):
    return pl.CostEstimate(flops=int(flops), bytes_accessed=int(moved), transcendentals=0)


def ring_order(holders):
    columns = 1
    while 2 * (columns * 2) ** 2 <= holders:
        columns *= 2
    columns = max(columns, 2) if holders >= 4 else 1
    rows = holders // columns
    order = [row * columns for row in range(rows)]
    for back, row in enumerate(reversed(range(rows))):
        line = range(1, columns) if back % 2 == 0 else reversed(range(1, columns))
        order += [row * columns + column for column in line]
    return order


def norm_kernel(parts, experts, own_ref, gain_ref, router_ref, *refs):
    count = len(parts)
    token_refs, route_refs = refs[: len(sum(parts, []))], refs[len(sum(parts, [])) : -2]
    normed_ref, weight_ref = refs[-2:]
    gain = gain_ref[...].astype(jnp.float32)
    base = 0
    flat = 0
    for block in range(count):
        start = base
        for _ in parts[block]:
            rows = token_refs[flat].shape[0]
            for at in range(0, rows, 32):
                values = token_refs[flat][at : at + 32, :].astype(jnp.float32)
                square = jnp.mean(values * values, axis=-1, keepdims=True)
                normed = values * lax.rsqrt(square + 1e-06) * gain
                normed_ref[base + at : base + at + 32, :] = normed.astype(jnp.bfloat16)
            base += rows
            flat += 1
        rows = base - start
        logits = jnp.dot(
            normed_ref[start:base, :], router_ref[...], preferred_element_type=jnp.float32
        )
        routes = route_refs[block][...]
        lanes = lax.broadcasted_iota(jnp.int32, (rows, rows), 0)
        named = lanes == routes[0:1, :]
        for choice in range(1, routes.shape[0]):
            named = named | (lanes == routes[choice : choice + 1, :])
        named = jnp.where(named, 1.0, 0.0).T[:, :experts]
        picked = jax.nn.sigmoid(logits) * named
        total = jnp.sum(picked, axis=1, keepdims=True)
        mine = jnp.sum(picked * own_ref[...], axis=1, keepdims=True) / total
        chosen = jnp.sum(named * own_ref[...], axis=1, keepdims=True)
        weight = jnp.where(chosen > 0, mine, 0.0)
        weight_ref[start:base, :] = jnp.broadcast_to(weight, (rows, 128))


def norm_blocks(own, gain, router, tokens, routes):
    parts = [[0] * len(block) for block in tokens]
    rows = sum(part.shape[0] for block in tokens for part in block)
    width = gain.shape[1]
    flat = [part for block in tokens for part in block]
    return pl.pallas_call(
        functools.partial(norm_kernel, parts, router.shape[1]),
        out_shape=(
            jax.ShapeDtypeStruct((rows, width), jnp.bfloat16),
            jax.ShapeDtypeStruct((rows, 128), jnp.float32),
        ),
        in_specs=[WHOLE] * (3 + len(flat) + len(routes)),
        out_specs=(WHOLE, WHOLE),
        compiler_params=params(),
        cost_estimate=cost(rows * width * 16, rows * width * 4),
        name="norm_gate",
    )(own, gain, router, *flat, *routes)


def fetch(me, refs, target, sems, first):
    copies = []
    depth = refs[0].shape[0]
    for apart, ref in enumerate(refs):
        at = pl.multiple_of((me ^ apart) * depth, depth)
        copies.append(
            pltpu.make_async_copy(ref, target.at[pl.ds(at, depth), :], sems.at[first + apart])
        )
        copies[-1].start()
    return copies


def hidden_kernel(inputs, pieces, me_ref, *refs):
    normed, weight = refs[:inputs], refs[inputs : 2 * inputs]
    gates = refs[2 * inputs : 2 * inputs + pieces]
    uppers = refs[2 * inputs + pieces : 2 * inputs + 2 * pieces]
    outs = refs[2 * inputs + 2 * pieces : 3 * inputs + 2 * pieces]
    gate_mat, upper_mat, sems = refs[3 * inputs + 2 * pieces :]
    me = me_ref[0]
    gate_copies = fetch(me, gates, gate_mat, sems, 0)
    upper_copies = fetch(me, uppers, upper_mat, sems, pieces)
    for copy in gate_copies:
        copy.wait()
    for copy in upper_copies:
        copy.wait()
    for at in range(inputs):
        rows = normed[at][...]
        gate = jnp.dot(rows, gate_mat[...], preferred_element_type=jnp.float32)
        upper = jnp.dot(rows, upper_mat[...], preferred_element_type=jnp.float32)
        scale = weight[at][:, :1]
        outs[at][...] = jnp.where(
            scale > 0, jnp.maximum(gate, 0.0) * upper * scale, 0.0
        ).astype(jnp.bfloat16)


def hidden_blocks(me, normed, weight, gates, uppers):
    pieces = len(gates)
    width, units = gates[0].shape[0] * pieces, gates[0].shape[1]
    rows = sum(block.shape[0] for block in normed)
    return pl.pallas_call(
        functools.partial(hidden_kernel, len(normed), pieces),
        out_shape=tuple(
            jax.ShapeDtypeStruct((block.shape[0], units), jnp.bfloat16) for block in normed
        ),
        in_specs=[SCALAR] + [WHOLE] * (2 * len(normed)) + [ANYWHERE] * (2 * pieces),
        out_specs=tuple(WHOLE for _ in normed),
        scratch_shapes=[
            pltpu.VMEM((width, units), jnp.bfloat16),
            pltpu.VMEM((width, units), jnp.bfloat16),
            pltpu.SemaphoreType.DMA((2 * pieces,)),
        ],
        compiler_params=params(),
        cost_estimate=cost(4 * rows * width * units, 4 * width * units),
        name="hidden",
    )(me, *normed, *weight, *gates, *uppers)


def down_kernel(counts, pieces, me_ref, *refs):
    inputs = len(counts)
    hidden = refs[:inputs]
    downs = refs[inputs : inputs + pieces]
    outs = refs[inputs + pieces : inputs + pieces + sum(counts)]
    down_mat, sems = refs[inputs + pieces + sum(counts) :]
    for copy in fetch(me_ref[0], downs, down_mat, sems, 0):
        copy.wait()
    at = 0
    for block, count in enumerate(counts):
        out = jnp.dot(hidden[block][...], down_mat[...], preferred_element_type=jnp.float32)
        rows = out.shape[0] // count
        for part in range(count):
            outs[at][...] = out[part * rows : (part + 1) * rows, :].astype(outs[at].dtype)
            at += 1


def down_blocks(me, hidden, counts, kinds, downs):
    pieces = len(downs)
    units, width = downs[0].shape[0] * pieces, downs[0].shape[1]
    shapes = []
    for block, count in zip(hidden, counts):
        shapes += [(block.shape[0] // count, width)] * count
    rows = sum(shape[0] for shape in shapes)
    return pl.pallas_call(
        functools.partial(down_kernel, counts, pieces),
        out_shape=tuple(jax.ShapeDtypeStruct(s, kind) for s, kind in zip(shapes, kinds)),
        in_specs=[SCALAR] + [WHOLE] * len(hidden) + [ANYWHERE] * pieces,
        out_specs=tuple(WHOLE for _ in shapes),
        scratch_shapes=[
            pltpu.VMEM((units, width), jnp.bfloat16),
            pltpu.SemaphoreType.DMA((pieces,)),
        ],
        compiler_params=params(),
        cost_estimate=cost(2 * rows * width * units, 2 * width * units + 4 * rows * width),
        name="down",
    )(me, *hidden, *downs)


def gather_blk(piece):
    size = lax.axis_size("blk")
    have = {0: piece}
    bit = size // 2
    while bit:
        pairs = [(i, i ^ bit) for i in range(size)]
        have.update({k ^ bit: lax.ppermute(v, "blk", pairs) for k, v in list(have.items())})
        bit //= 2
    return [have[k] for k in range(size)]


def add_round(*terms):
    total = terms[0].astype(jnp.float32)
    for term in terms[1:]:
        total = total + term.astype(jnp.float32)
    return total.astype(jnp.bfloat16)


def on_device(
    tokens, norm_gain, router_weight, routes, placement, gate_weight, up_weight, down_weight
):
    holders = lax.axis_size("ep")
    tok_rows, width = tokens.shape
    far = holders // 2
    order = ring_order(holders)
    ahead = [(order[i], order[(i + 1) % holders]) for i in range(holders)]
    behind = [(target, source) for source, target in ahead]

    def clock(x):
        return lax.ppermute(x, "ep", ahead)

    def counter(x):
        return lax.ppermute(x, "ep", behind)

    me = lax.axis_index("blk").astype(jnp.int32).reshape(1)
    own = (placement == lax.axis_index("ep")).astype(jnp.float32)[None, :]
    gain = norm_gain[None, :]
    gates = gather_blk(gate_weight[0])
    uppers = gather_blk(up_weight[0])
    half = width // 2
    downs = [gather_blk(down_weight[0][:, :half]), gather_blk(down_weight[0][:, half:])]

    names = routes.T
    cut = tok_rows // 2
    from_behind, from_ahead = [tokens], [tokens]
    names_behind, names_ahead = [names], [names]
    for step in range(1, far):
        from_behind.append(clock(from_behind[-1]))
        names_behind.append(clock(names_behind[-1]))
        from_ahead.append(counter(from_ahead[-1]))
        names_ahead.append(counter(names_ahead[-1]))
    far_parts = [clock(from_behind[-1][:cut]), counter(from_ahead[-1][cut:])]
    far_names = clock(names_behind[-1])

    def norm(blocks, block_names):
        return norm_blocks(own, gain, router_weight, blocks, block_names)

    stages = [norm([[tokens]], [names])]
    for step in range(1, far):
        stages.append(
            norm(
                [[from_behind[step]], [from_ahead[step]]],
                [names_behind[step], names_ahead[step]],
            )
        )
    stages.append(norm([far_parts], [far_names]))

    hidden = []
    groups = [stages[:3]] + [stages[at : at + 2] for at in range(3, len(stages), 2)]
    for group in groups:
        hidden += hidden_blocks(
            me, [normed for normed, _ in group], [w for _, w in group], gates, uppers
        )

    results = []
    for side, down in enumerate(downs):
        long_way, short_way = (clock, counter) if side == 0 else (counter, clock)
        to_behind, to_ahead = {}, {}
        for at in range(0, len(hidden), 5):
            chosen = list(range(at, min(at + 5, len(hidden))))
            counts = [1 if step in (0, far) else 2 for step in chosen]
            kinds, slots = [], []
            for step in chosen:
                if step in (0, far):
                    kinds.append(jnp.bfloat16 if step == far else jnp.float32)
                    slots.append((to_behind, step))
                else:
                    first_behind = side == 0 and step == far - 1
                    first_ahead = side == 1 and step == far - 1
                    kinds += [
                        jnp.bfloat16 if first_behind else jnp.float32,
                        jnp.bfloat16 if first_ahead else jnp.float32,
                    ]
                    slots += [(to_behind, step), (to_ahead, step)]
            outs = down_blocks(me, [hidden[step] for step in chosen], counts, kinds, down)
            for (table, step), out in zip(slots, outs):
                table[step] = out
        long_sums, short_sums = (to_ahead, to_behind) if side == 0 else (to_behind, to_ahead)
        long_run = long_way(to_behind[far])
        short_run = short_way(short_sums[far - 1])
        for step in range(far - 1, 0, -1):
            long_run = long_way(add_round(long_run, long_sums[step]))
            if step > 1:
                short_run = short_way(add_round(short_run, short_sums[step - 1]))
        results.append(add_round(to_behind[0], long_run, short_run))
    return jnp.concatenate(results, axis=1)


def solution(mesh):
    in_specs = (
        P(("ep", "blk"), None),
        P(),
        P(),
        P(("ep", "blk"), None),
        P(),
        P("ep", "blk", None),
        P("ep", "blk", None),
        P("ep", "blk", None),
    )
    out_specs = P(("ep", "blk"), None)
    return jax.shard_map(
        on_device, mesh=mesh, in_specs=in_specs, out_specs=out_specs, check_vma=False
    )
```

```python
import functools

import jax
import jax.numpy as jnp
from jax import lax
from jax.experimental import pallas as pl
from jax.experimental.pallas import tpu as pltpu
from jax.sharding import PartitionSpec as P

VMEM_LIMIT = 28 * 1024 * 1024
MOST_VMEM = 60 * 1024 * 1024
MUCH_VMEM = 54 * 1024 * 1024
EXTRA = 128
WHOLE = pl.BlockSpec(memory_space=pltpu.VMEM)
SCALAR = pl.BlockSpec(memory_space=pltpu.SMEM)
ANYWHERE = pl.BlockSpec(memory_space=pl.ANY)


def params(limit=VMEM_LIMIT):
    return pltpu.CompilerParams(vmem_limit_bytes=limit)


def cost(flops, moved):
    return pl.CostEstimate(flops=int(flops), bytes_accessed=int(moved), transcendentals=0)


def ring_order(holders):
    columns = 1
    while 2 * (columns * 2) ** 2 <= holders:
        columns *= 2
    columns = max(columns, 2) if holders >= 4 else 1
    rows = holders // columns
    order = [row * columns for row in range(rows)]
    for back, row in enumerate(reversed(range(rows))):
        line = range(1, columns) if back % 2 == 0 else reversed(range(1, columns))
        order += [row * columns + column for column in line]
    return order


def after_kernel(*refs):
    pass


def after(place, value, *others):
    marks = [other[:8, :128] for other in others]
    return pl.pallas_call(
        after_kernel,
        out_shape=jax.ShapeDtypeStruct(value.shape, value.dtype),
        in_specs=[place] + [WHOLE] * len(marks),
        out_specs=place,
        input_output_aliases={0: 0},
        compiler_params=params(),
        cost_estimate=cost(0, 4096),
        name="after",
    )(value, *marks)


def pack_kernel(experts, *refs):
    sources, (out_ref, pair_ref, gain_ref, router_ref, routes_ref, token_ref, sems) = refs[:6], refs[6:]
    depth = sources[4].shape[0]
    targets = [gain_ref, router_ref, routes_ref, token_ref]
    targets += [pair_ref.at[:depth, :], pair_ref.at[depth:, :]]
    copies = [
        pltpu.make_async_copy(source, target, sems.at[at])
        for at, (source, target) in enumerate(zip(sources, targets))
    ]
    for copy in copies:
        copy.start()
    for copy in copies[:4]:
        copy.wait()
    rows, width = token_ref.shape
    gain = gain_ref[...].astype(jnp.float32)[None, :]
    for at in range(0, rows, 32):
        values = token_ref[at : at + 32, :].astype(jnp.float32)
        square = jnp.mean(values * values, axis=-1, keepdims=True)
        normed = values * lax.rsqrt(square + 1e-06) * gain
        out_ref[at : at + 32, :width] = normed.astype(jnp.bfloat16)
    logits = lax.dot_general(
        out_ref[:, :width],
        router_ref[...],
        (((1,), (1,)), ((), ())),
        preferred_element_type=jnp.float32,
    )
    routes = routes_ref[...]
    lanes = lax.broadcasted_iota(jnp.int32, (128, rows), 0)
    named = lanes == routes[0:1, :]
    for choice in range(1, routes.shape[0]):
        named = named | (lanes == routes[choice : choice + 1, :])
    named = jnp.where(named, 1.0, 0.0).T[:, :experts] > 0
    picked = jnp.where(named, jax.nn.sigmoid(logits), 0.0)
    weight = picked / jnp.sum(picked, axis=1, keepdims=True)
    weight = jnp.where(named, weight, 0.0)
    high = weight.astype(jnp.bfloat16)
    low = (weight - high.astype(jnp.float32)).astype(jnp.bfloat16)
    spare = jnp.zeros((rows, EXTRA - 2 * experts), jnp.bfloat16)
    out_ref[:, width:] = jnp.concatenate([high, low, spare], axis=1)
    for copy in copies[4:]:
        copy.wait()


def pack(gain, router, names, tokens, gate, upper):
    rows, width = tokens.shape
    depth, units = gate.shape
    small = [gain, router, names, tokens]
    return pl.pallas_call(
        functools.partial(pack_kernel, router.shape[0]),
        out_shape=(
            jax.ShapeDtypeStruct((rows, width + EXTRA), jnp.bfloat16),
            jax.ShapeDtypeStruct((2 * depth, units), jnp.bfloat16),
        ),
        in_specs=[ANYWHERE] * 6,
        out_specs=(WHOLE, WHOLE),
        scratch_shapes=[pltpu.VMEM(x.shape, x.dtype) for x in small]
        + [pltpu.SemaphoreType.DMA((6,))],
        compiler_params=params(MOST_VMEM),
        cost_estimate=cost(rows * width * 16, rows * width * 4 + 8 * depth * units),
        name="pack",
    )(*small, gate, upper)


def fetch(me, refs, first, columns, target, sems):
    depth = target.shape[0] // len(refs)
    copies = []
    for apart, ref in enumerate(refs):
        at = pl.multiple_of((me ^ apart) * depth, depth)
        source = ref.at[pl.ds(first, depth), columns]
        copy = pltpu.make_async_copy(source, target.at[pl.ds(at, depth), :], sems.at[apart])
        copy.start()
        copies.append(copy)
    return copies


def hidden_rows(rows, own_ref, gate_mat, upper_mat, ready=()):
    width = gate_mat.shape[0]
    scale = jnp.sum(rows[:, width:].astype(jnp.float32) * own_ref[...], axis=1, keepdims=True)
    gate = jnp.dot(rows[:, :width], gate_mat[...], preferred_element_type=jnp.float32)
    for copy in ready:
        copy.wait()
    upper = jnp.dot(rows[:, :width], upper_mat[...], preferred_element_type=jnp.float32)
    hidden = jnp.where(scale > 0, jnp.maximum(gate, 0.0) * upper * scale, 0.0)
    return hidden.astype(jnp.bfloat16)


def first_hidden_kernel(inputs, pieces, me_ref, own_ref, *refs):
    blocks, weights = refs[:inputs], refs[inputs : inputs + pieces]
    outs, scratch = refs[inputs + pieces : -4], refs[-4:]
    outs, (gate_mat, upper_mat) = outs[:-2], outs[-2:]
    rows_ref, gate_sems, upper_sems, row_sems = scratch
    width, units = gate_mat.shape
    columns = pl.ds(0, units)
    row_copies, at = [], 0
    for place, block in enumerate(blocks):
        target = rows_ref.at[at : at + block.shape[0], :]
        row_copies.append(pltpu.make_async_copy(block, target, row_sems.at[place]))
        at += block.shape[0]
    for copy in row_copies:
        copy.start()
    gate_copies = fetch(me_ref[0], weights, 0, columns, gate_mat, gate_sems)
    upper_copies = fetch(me_ref[0], weights, width // pieces, columns, upper_mat, upper_sems)
    for copy in row_copies + gate_copies:
        copy.wait()
    at = 0
    for out in outs:
        rows = rows_ref[at : at + out.shape[0], :]
        ready = () if at else upper_copies
        out[...] = hidden_rows(rows, own_ref, gate_mat, upper_mat, ready)
        at += out.shape[0]


def first_hidden_blocks(me, own, groups, pairs):
    pieces = len(pairs)
    width, units = pairs[0].shape[0] // 2 * pieces, pairs[0].shape[1]
    heights = [sum(block.shape[0] for block in group) for group in groups]
    blocks = [block for group in groups for block in group]
    shapes = [(height, units) for height in heights] + [(width, units)] * 2
    return pl.pallas_call(
        functools.partial(first_hidden_kernel, len(blocks), pieces),
        out_shape=tuple(jax.ShapeDtypeStruct(shape, jnp.bfloat16) for shape in shapes),
        in_specs=[SCALAR, WHOLE] + [ANYWHERE] * (len(blocks) + pieces),
        out_specs=tuple(WHOLE for _ in shapes),
        scratch_shapes=[
            pltpu.VMEM((sum(heights), width + EXTRA), jnp.bfloat16),
            pltpu.SemaphoreType.DMA((pieces,)),
            pltpu.SemaphoreType.DMA((pieces,)),
            pltpu.SemaphoreType.DMA((len(blocks),)),
        ],
        compiler_params=params(MUCH_VMEM),
        name="first_hidden",
    )(me, own, *blocks, *pairs)


def hidden_kernel(counts, own_ref, gate_mat, upper_mat, *refs):
    outs, at = refs[sum(counts) :], 0
    for count, out in zip(counts, outs):
        group = [block[...] for block in refs[at : at + count]]
        at += count
        rows = jnp.concatenate(group, axis=0) if count > 1 else group[0]
        out[...] = hidden_rows(rows, own_ref, gate_mat, upper_mat)


def hidden_blocks(own, groups, gate_mat, upper_mat):
    width, units = gate_mat.shape
    heights = [sum(block.shape[0] for block in group) for group in groups]
    blocks = [block for group in groups for block in group]
    return pl.pallas_call(
        functools.partial(hidden_kernel, [len(group) for group in groups]),
        out_shape=tuple(jax.ShapeDtypeStruct((h, units), jnp.bfloat16) for h in heights),
        in_specs=[WHOLE] * (3 + len(blocks)),
        out_specs=tuple(WHOLE for _ in groups),
        compiler_params=params(),
        name="hidden",
    )(own, gate_mat, upper_mat, *blocks)


def down_kernel(slots, pieces, column, me_ref, *refs):
    inputs = len(slots)
    hidden = refs[:inputs]
    outs = refs[inputs + pieces : -2]
    down_mat, sems = refs[-2:]
    columns = pl.ds(column, down_mat.shape[1])
    for copy in fetch(me_ref[0], refs[inputs : inputs + pieces], 0, columns, down_mat, sems):
        copy.wait()
    for group, parts in zip(hidden, slots):
        out = jnp.dot(group[...], down_mat[...], preferred_element_type=jnp.float32)
        at = 0
        for slot, first, count in parts:
            part = out[at : at + count, :]
            outs[slot][first : first + count, :] = part.astype(outs[slot].dtype)
            at += count


def down_blocks(me, column, width, hidden, slots, kinds, downs):
    pieces = len(downs)
    units = downs[0].shape[0] * pieces
    flat = [part for parts in slots for part in parts]
    heights = [sum(c for slot, _, c in flat if slot == at) for at in range(len(kinds))]
    rows = sum(heights)
    return pl.pallas_call(
        functools.partial(down_kernel, slots, pieces, column),
        out_shape=tuple(
            jax.ShapeDtypeStruct((height, width), kind) for height, kind in zip(heights, kinds)
        ),
        in_specs=[SCALAR] + [WHOLE] * len(hidden) + [ANYWHERE] * pieces,
        out_specs=tuple(WHOLE for _ in kinds),
        scratch_shapes=[
            pltpu.VMEM((units, width), jnp.bfloat16),
            pltpu.SemaphoreType.DMA((pieces,)),
        ],
        compiler_params=params(),
        cost_estimate=cost(2 * rows * width * units, 2 * width * units + 4 * rows * width),
        name="down",
    )(me, *hidden, *downs)


def swap_blk(value, bit):
    pairs = [(i, i ^ bit) for i in range(lax.axis_size("blk"))]
    return lax.ppermute(value, "blk", pairs)


def outer_rounds(piece):
    have = {0: piece}
    bit = lax.axis_size("blk") // 2
    while bit > 1:
        have.update({k ^ bit: swap_blk(value, bit) for k, value in list(have.items())})
        bit //= 2
    return have


def last_round(have, *others):
    have = {k: after(ANYWHERE, value, *others) if k else value for k, value in have.items()}
    have.update({k ^ 1: swap_blk(value, 1) for k, value in list(have.items())})
    return [have[k] for k in sorted(have)]


def add_round(*terms):
    total = terms[0].astype(jnp.float32)
    for term in terms[1:]:
        total = total + term.astype(jnp.float32)
    return total.astype(jnp.bfloat16)


def on_device(
    tokens, norm_gain, router_weight, routes, placement, gate_weight, up_weight, down_weight
):
    holders = lax.axis_size("ep")
    tok_rows, width = tokens.shape
    far = holders // 2
    order = ring_order(holders)
    ahead = [(order[i], order[(i + 1) % holders]) for i in range(holders)]
    behind = [(target, source) for source, target in ahead]

    def clock(x):
        return lax.ppermute(x, "ep", ahead)

    def counter(x):
        return lax.ppermute(x, "ep", behind)

    me = lax.axis_index("blk").astype(jnp.int32).reshape(1)
    experts = router_weight.shape[1]
    held = (placement == lax.axis_index("ep")).astype(jnp.float32)
    own = jnp.pad(jnp.concatenate([held, held]), (0, EXTRA - 2 * experts))[None, :]

    packed, pair = pack(
        norm_gain, router_weight.T, routes.T, tokens, gate_weight[0], up_weight[0]
    )
    pairs = outer_rounds(pair)
    half = width // 2
    downs = outer_rounds(down_weight[0])

    cut = tok_rows // 2
    from_behind, from_ahead = [packed], [packed]
    for step in range(1, far):
        from_behind.append(clock(from_behind[-1]))
        from_ahead.append(counter(from_ahead[-1]))
    far_parts = [clock(from_behind[-1][:cut]), counter(from_ahead[-1][cut:])]

    pairs = last_round(pairs, from_behind[far - 1], from_ahead[far - 1])

    groups = [[((0, 0), 0, packed)]]
    for step in range(1, far):
        groups.append([((-1, step), 0, from_behind[step]), ((1, step), 0, from_ahead[step])])
    groups.append([((0, far), 0, far_parts[0]), ((0, far), cut, far_parts[1])])
    def only_blocks(chosen):
        return [[block for _, _, block in group] for group in chosen]

    *hidden, gate_mat, upper_mat = first_hidden_blocks(me, own, only_blocks(groups[:3]), pairs)
    first_done = hidden[-1]
    for low in range(3, len(groups), 2):
        blocks = only_blocks(groups[low : low + 2])
        blocks[-1] = [after(WHOLE, block, first_done) for block in blocks[-1]]
        hidden += hidden_blocks(own, blocks, gate_mat, upper_mat)

    downs = last_round(downs, hidden[-1])
    results = []
    for side in range(2):
        long_way, short_way = (clock, counter) if side == 0 else (counter, clock)
        long_sign = 1 if side == 0 else -1
        sent_first = [(0, far), (-long_sign, far - 1)]
        table = {}
        for low in range(0, len(hidden), 5):
            chosen = groups[low : low + 5]
            keys = list(dict.fromkeys(key for group in chosen for key, _, _ in group))
            kinds = [jnp.bfloat16 if key in sent_first else jnp.float32 for key in keys]
            slots = [
                [(keys.index(key), first, block.shape[0]) for key, first, block in group]
                for group in chosen
            ]
            outs = down_blocks(me, side * half, half, hidden[low : low + 5], slots, kinds, downs)
            table.update(zip(keys, outs))
        long_run = long_way(table[0, far])
        short_run = short_way(table[-long_sign, far - 1])
        for step in range(far - 1, 0, -1):
            long_run = long_way(add_round(long_run, table[long_sign, step]))
            if step > 1:
                short_run = short_way(add_round(short_run, table[-long_sign, step - 1]))
        results.append(add_round(table[0, 0], long_run, short_run))
    return jnp.concatenate(results, axis=1)


def solution(mesh):
    in_specs = (
        P(("ep", "blk"), None),
        P(),
        P(),
        P(("ep", "blk"), None),
        P(),
        P("ep", "blk", None),
        P("ep", "blk", None),
        P("ep", "blk", None),
    )
    out_specs = P(("ep", "blk"), None)
    return jax.shard_map(
        on_device, mesh=mesh, in_specs=in_specs, out_specs=out_specs, check_vma=False
    )
```

```python
import functools

import jax
import jax.numpy as jnp
from jax import lax
from jax.experimental import pallas as pl
from jax.experimental.pallas import tpu as pltpu
from jax.sharding import PartitionSpec as P

VMEM_LIMIT = 28 * 1024 * 1024
MOST_VMEM = 60 * 1024 * 1024
MUCH_VMEM = 52 * 1024 * 1024
EXTRA = 128
WHOLE = pl.BlockSpec(memory_space=pltpu.VMEM)
SCALAR = pl.BlockSpec(memory_space=pltpu.SMEM)
ANYWHERE = pl.BlockSpec(memory_space=pl.ANY)


def params(limit=VMEM_LIMIT):
    return pltpu.CompilerParams(vmem_limit_bytes=limit)


def cost(flops, moved):
    return pl.CostEstimate(flops=int(flops), bytes_accessed=int(moved), transcendentals=0)


def ring_order(holders):
    columns = 1
    while 2 * (columns * 2) ** 2 <= holders:
        columns *= 2
    columns = max(columns, 2) if holders >= 4 else 1
    rows = holders // columns
    order = [row * columns for row in range(rows)]
    for back, row in enumerate(reversed(range(rows))):
        line = range(1, columns) if back % 2 == 0 else reversed(range(1, columns))
        order += [row * columns + column for column in line]
    return order


def after_kernel(count, value_ref, *refs):
    outs = refs[len(refs) - count :]
    rows = outs[0].shape[0]
    for at, out in enumerate(outs):
        out[...] = value_ref[at * rows : (at + 1) * rows, :]


def after(value, count, *others):
    marks = [other[:8, :128] for other in others]
    part = jax.ShapeDtypeStruct((value.shape[0] // count, value.shape[1]), value.dtype)
    return pl.pallas_call(
        functools.partial(after_kernel, count),
        out_shape=(part,) * count,
        in_specs=[WHOLE] * (1 + len(marks)),
        out_specs=(WHOLE,) * count,
        compiler_params=params(),
        name="after",
    )(value, *marks)


def pack_kernel(experts, *refs):
    sources, (out_ref, pair_ref, gain_ref, router_ref, routes_ref, token_ref, sems) = refs[:6], refs[6:]
    depth = sources[4].shape[0]
    targets = [gain_ref, router_ref, routes_ref, token_ref]
    targets += [pair_ref.at[:depth, :], pair_ref.at[depth:, :]]
    copies = [
        pltpu.make_async_copy(source, target, sems.at[at])
        for at, (source, target) in enumerate(zip(sources, targets))
    ]
    for copy in copies:
        copy.start()
    for copy in copies[:4]:
        copy.wait()
    rows, width = token_ref.shape
    gain = gain_ref[...].astype(jnp.float32)[None, :]
    for at in range(0, rows, 32):
        values = token_ref[at : at + 32, :].astype(jnp.float32)
        square = jnp.mean(values * values, axis=-1, keepdims=True)
        normed = values * lax.rsqrt(square + 1e-06) * gain
        out_ref[at : at + 32, :width] = normed.astype(jnp.bfloat16)
    logits = lax.dot_general(
        out_ref[:, :width],
        router_ref[...],
        (((1,), (1,)), ((), ())),
        preferred_element_type=jnp.float32,
    )
    routes = routes_ref[...]
    lanes = lax.broadcasted_iota(jnp.int32, (128, rows), 0)
    named = lanes == routes[0:1, :]
    for choice in range(1, routes.shape[0]):
        named = named | (lanes == routes[choice : choice + 1, :])
    named = jnp.where(named, 1.0, 0.0).T[:, :experts] > 0
    picked = jnp.where(named, jax.nn.sigmoid(logits), 0.0)
    weight = picked / jnp.sum(picked, axis=1, keepdims=True)
    weight = jnp.where(named, weight, 0.0)
    high = weight.astype(jnp.bfloat16)
    low = (weight - high.astype(jnp.float32)).astype(jnp.bfloat16)
    spare = jnp.zeros((rows, EXTRA - 2 * experts), jnp.bfloat16)
    out_ref[:, width:] = jnp.concatenate([high, low, spare], axis=1)
    for copy in copies[4:]:
        copy.wait()


def pack(gain, router, names, tokens, gate, upper):
    rows, width = tokens.shape
    depth, units = gate.shape
    small = [gain, router, names, tokens]
    return pl.pallas_call(
        functools.partial(pack_kernel, router.shape[0]),
        out_shape=(
            jax.ShapeDtypeStruct((rows, width + EXTRA), jnp.bfloat16),
            jax.ShapeDtypeStruct((2 * depth, units), jnp.bfloat16),
        ),
        in_specs=[ANYWHERE] * 6,
        out_specs=(WHOLE, WHOLE),
        scratch_shapes=[pltpu.VMEM(x.shape, x.dtype) for x in small]
        + [pltpu.SemaphoreType.DMA((6,))],
        compiler_params=params(MOST_VMEM),
        cost_estimate=cost(rows * width * 16, rows * width * 4 + 8 * depth * units),
        name="pack",
    )(*small, gate, upper)


def assemble(me, pieces, first, columns, target):
    depth = target.shape[0] // len(pieces)
    for apart, parts in enumerate(pieces):
        at = pl.multiple_of((me ^ apart) * depth, depth)
        begin = 0
        for part in parts:
            end = begin + part.shape[0]
            low, high = max(begin, first), min(end, first + depth)
            if low < high:
                place = pl.ds(pl.multiple_of(at + (low - first), 16), high - low)
                target[place, :] = part[low - begin : high - begin, columns]
            begin = end


def take_pieces(layout, refs):
    pieces, at = [], 0
    for count in layout:
        pieces.append(refs[at : at + count])
        at += count
    return pieces, refs[at:]


def stacked(pieces, first, depth):
    found = []
    for parts in pieces:
        begin = 0
        for part in parts:
            end = begin + part.shape[0]
            low, high = max(begin, first), min(end, first + depth)
            if low < high:
                found.append(part[low - begin : high - begin, :])
            begin = end
    return jnp.concatenate(found, axis=0)


def hidden_kernel(inputs, layout, me_ref, place_ref, *refs):
    blocks, refs = refs[:inputs], refs[inputs:]
    pieces, refs = take_pieces(layout, refs)
    outs, (rows_ref, gate_mat, upper_mat, sems) = refs[:-4], refs[-4:]
    width = rows_ref.shape[1] - EXTRA
    depth = width // len(pieces)
    in_place = depth % 128 == 0
    copies, at = [], 0
    for place, block in enumerate(blocks):
        target = rows_ref.at[at : at + block.shape[0], :]
        copies.append(pltpu.make_async_copy(block, target, sems.at[place]))
        copies[-1].start()
        at += block.shape[0]
    if not in_place:
        columns = slice(0, gate_mat.shape[1])
        assemble(me_ref[0], pieces, 0, columns, gate_mat)
        assemble(me_ref[0], pieces, depth, columns, upper_mat)
    lanes = lax.broadcasted_iota(jnp.int32, (1, EXTRA), 1)
    own = jnp.zeros((1, EXTRA), jnp.float32)
    experts = place_ref.shape[0]
    for expert in range(experts):
        mine = ((lanes == expert) | (lanes == expert + experts)) & (place_ref[expert] == me_ref[1])
        own = jnp.where(mine, 1.0, own)
    at, done, fetched = 0, 0, 0
    for out in outs:
        here = slice(at, at + out.shape[0])
        at += out.shape[0]
        while fetched < at:
            copies[done].wait()
            fetched += blocks[done].shape[0]
            done += 1
        weights = rows_ref[here, width:].astype(jnp.float32)
        scale = jnp.sum(weights * own, axis=1, keepdims=True)
        if in_place:
            rows = [
                rows_ref[here, pl.ds(pl.multiple_of((me_ref[0] ^ apart) * depth, depth), depth)]
                for apart in range(len(pieces))
            ]
            rows = jnp.concatenate(rows, axis=1)
            first, second = stacked(pieces, 0, depth), stacked(pieces, depth, depth)
        else:
            rows, first, second = rows_ref[here, :width], gate_mat[...], upper_mat[...]
        gate = jnp.dot(rows, first, preferred_element_type=jnp.float32)
        upper = jnp.dot(rows, second, preferred_element_type=jnp.float32)
        hidden = jnp.where(scale > 0, jnp.maximum(gate, 0.0) * upper * scale, 0.0)
        out[...] = hidden.astype(jnp.bfloat16)


def hidden_blocks(me, placement, groups, pairs):
    layout = [len(parts) for parts in pairs]
    flat = [part for parts in pairs for part in parts]
    width, units = sum(part.shape[0] for part in flat) // 2, flat[0].shape[1]
    heights = [sum(block.shape[0] for block in group) for group in groups]
    blocks = [block for group in groups for block in group]
    whole = (width, units) if width // len(pairs) % 128 else (16, 128)
    return pl.pallas_call(
        functools.partial(hidden_kernel, len(blocks), layout),
        out_shape=tuple(jax.ShapeDtypeStruct((h, units), jnp.bfloat16) for h in heights),
        in_specs=[SCALAR, SCALAR] + [ANYWHERE] * len(blocks) + [WHOLE] * len(flat),
        out_specs=tuple(WHOLE for _ in groups),
        scratch_shapes=[
            pltpu.VMEM((sum(heights), width + EXTRA), jnp.bfloat16),
            pltpu.VMEM(whole, jnp.bfloat16),
            pltpu.VMEM(whole, jnp.bfloat16),
            pltpu.SemaphoreType.DMA((len(blocks),)),
        ],
        compiler_params=params(MUCH_VMEM),
        name="hidden",
    )(me, placement, *blocks, *flat)


def down_kernel(slots, layout, column, me_ref, *refs):
    hidden, refs = refs[: len(slots)], refs[len(slots) :]
    pieces, refs = take_pieces(layout, refs)
    outs, down_mat = refs[:-1], refs[-1]
    assemble(me_ref[0], pieces, 0, slice(column, column + down_mat.shape[1]), down_mat)
    for group, parts in zip(hidden, slots):
        out = jnp.dot(group[...], down_mat[...], preferred_element_type=jnp.float32)
        at = 0
        for slot, first, count in parts:
            part = out[at : at + count, :]
            outs[slot][first : first + count, :] = part.astype(outs[slot].dtype)
            at += count


def down_blocks(me, column, width, hidden, slots, kinds, downs):
    layout = [len(parts) for parts in downs]
    pieces = [part for parts in downs for part in parts]
    units = sum(part.shape[0] for part in pieces)
    flat = [part for parts in slots for part in parts]
    heights = [sum(c for slot, _, c in flat if slot == at) for at in range(len(kinds))]
    return pl.pallas_call(
        functools.partial(down_kernel, slots, layout, column),
        out_shape=tuple(
            jax.ShapeDtypeStruct((height, width), kind) for height, kind in zip(heights, kinds)
        ),
        in_specs=[SCALAR] + [WHOLE] * (len(hidden) + len(pieces)),
        out_specs=tuple(WHOLE for _ in kinds),
        scratch_shapes=[pltpu.VMEM((units, width), jnp.bfloat16)],
        compiler_params=params(),
        name="down",
    )(me, *hidden, *pieces)


def swap_blk(value, bit):
    pairs = [(i, i ^ bit) for i in range(lax.axis_size("blk"))]
    return lax.ppermute(value, "blk", pairs)


def outer_rounds(piece):
    have = {0: piece}
    bit = lax.axis_size("blk") // 2
    while bit > 1:
        have.update({k ^ bit: swap_blk(value, bit) for k, value in list(have.items())})
        bit //= 2
    return have


def last_round(have, count, *others):
    have = {k: after(v, count, *others) if k else [v] for k, v in have.items()}
    have.update({k ^ 1: [swap_blk(part, 1) for part in parts] for k, parts in list(have.items())})
    return [have[k] for k in sorted(have)]


def add_round(*terms):
    total = terms[0].astype(jnp.float32)
    for term in terms[1:]:
        total = total + term.astype(jnp.float32)
    return total.astype(jnp.bfloat16)


def on_device(
    tokens, norm_gain, router_weight, routes, placement, gate_weight, up_weight, down_weight
):
    holders = lax.axis_size("ep")
    tok_rows, width = tokens.shape
    far = holders // 2
    order = ring_order(holders)
    ahead = [(order[i], order[(i + 1) % holders]) for i in range(holders)]
    behind = [(target, source) for source, target in ahead]

    def clock(x):
        return lax.ppermute(x, "ep", ahead)

    def counter(x):
        return lax.ppermute(x, "ep", behind)

    me = jnp.stack([lax.axis_index("blk"), lax.axis_index("ep")]).astype(jnp.int32)

    downs = outer_rounds(down_weight[0])
    packed, pair = pack(
        norm_gain, router_weight.T, routes.T, tokens, gate_weight[0], up_weight[0]
    )
    pairs = outer_rounds(pair)
    half = width // 2

    cut = tok_rows // 2
    from_behind, from_ahead = [packed], [packed]
    for step in range(1, far):
        from_ahead.append(counter(from_ahead[-1]))
        from_behind.append(clock(from_behind[-1]))
    far_parts = [clock(from_behind[-1][:cut]), counter(from_ahead[-1][cut:])]

    pairs = last_round(pairs, 4, from_behind[far - 1], from_ahead[far - 1])

    groups = [[((0, 0), 0, packed)]]
    for step in range(1, far):
        groups.append([((-1, step), 0, from_behind[step]), ((1, step), 0, from_ahead[step])])
    groups.append([((0, far), 0, far_parts[0]), ((0, far), cut, far_parts[1])])
    def only_blocks(chosen):
        return [[block for _, _, block in group] for group in chosen]

    hidden = []
    for low in range(0, len(groups), 5):
        hidden += hidden_blocks(me, placement, only_blocks(groups[low : low + 5]), pairs)
    downs = last_round(downs, 1, hidden[-1])
    results = []
    for side in range(2):
        long_way, short_way = (clock, counter) if side == 0 else (counter, clock)
        long_sign = 1 if side == 0 else -1
        sent_first = [(0, far), (-long_sign, far - 1)]
        table = {}
        for low in range(0, len(hidden), 5):
            chosen = groups[low : low + 5]
            keys = list(dict.fromkeys(key for group in chosen for key, _, _ in group))
            kinds = [jnp.bfloat16 if key in sent_first else jnp.float32 for key in keys]
            slots = [
                [(keys.index(key), first, block.shape[0]) for key, first, block in group]
                for group in chosen
            ]
            outs = down_blocks(me, side * half, half, hidden[low : low + 5], slots, kinds, downs)
            table.update(zip(keys, outs))
        long_run = long_way(table[0, far])
        short_run = short_way(table[-long_sign, far - 1])
        for step in range(far - 1, 0, -1):
            long_run = long_way(add_round(long_run, table[long_sign, step]))
            if step > 1:
                short_run = short_way(add_round(short_run, table[-long_sign, step - 1]))
        results.append(add_round(table[0, 0], long_run, short_run))
    return jnp.concatenate(results, axis=1)


def solution(mesh):
    in_specs = (
        P(("ep", "blk"), None),
        P(),
        P(),
        P(("ep", "blk"), None),
        P(),
        P("ep", "blk", None),
        P("ep", "blk", None),
        P("ep", "blk", None),
    )
    out_specs = P(("ep", "blk"), None)
    return jax.shard_map(
        on_device, mesh=mesh, in_specs=in_specs, out_specs=out_specs, check_vma=False
    )
```

```python
import functools

import jax
import jax.numpy as jnp
from jax import lax
from jax.experimental import pallas as pl
from jax.experimental.pallas import tpu as pltpu
from jax.sharding import PartitionSpec as P

VMEM_LIMIT = 28 * 1024 * 1024
MOST_VMEM = 60 * 1024 * 1024
MUCH_VMEM = 52 * 1024 * 1024
EXTRA = 128
WHOLE = pl.BlockSpec(memory_space=pltpu.VMEM)
SCALAR = pl.BlockSpec(memory_space=pltpu.SMEM)
ANYWHERE = pl.BlockSpec(memory_space=pl.ANY)


def params(limit=VMEM_LIMIT):
    return pltpu.CompilerParams(vmem_limit_bytes=limit)


def cost(flops, moved):
    return pl.CostEstimate(flops=int(flops), bytes_accessed=int(moved), transcendentals=0)


def ring_order(holders):
    columns = 1
    while 2 * (columns * 2) ** 2 <= holders:
        columns *= 2
    columns = max(columns, 2) if holders >= 4 else 1
    rows = holders // columns
    order = [row * columns for row in range(rows)]
    for back, row in enumerate(reversed(range(rows))):
        line = range(1, columns) if back % 2 == 0 else reversed(range(1, columns))
        order += [row * columns + column for column in line]
    return order


def after_kernel(count, value_ref, *refs):
    outs = refs[len(refs) - count :]
    rows = outs[0].shape[0]
    for at, out in enumerate(outs):
        out[...] = value_ref[at * rows : (at + 1) * rows, :]


def after(value, count, *others):
    marks = [other[:8, :128] for other in others]
    part = jax.ShapeDtypeStruct((value.shape[0] // count, value.shape[1]), value.dtype)
    return pl.pallas_call(
        functools.partial(after_kernel, count),
        out_shape=(part,) * count,
        in_specs=[WHOLE] * (1 + len(marks)),
        out_specs=(WHOLE,) * count,
        compiler_params=params(),
        name="after",
    )(value, *marks)


def pack_kernel(experts, *refs):
    sources, (out_ref, pair_ref, gain_ref, router_ref, routes_ref, token_ref, sems) = refs[:6], refs[6:]
    depth = sources[4].shape[0]
    targets = [gain_ref, router_ref, routes_ref, token_ref]
    targets += [pair_ref.at[:depth, :], pair_ref.at[depth:, :]]
    copies = [
        pltpu.make_async_copy(source, target, sems.at[at])
        for at, (source, target) in enumerate(zip(sources, targets))
    ]
    for copy in copies:
        copy.start()
    for copy in copies[:4]:
        copy.wait()
    rows, width = token_ref.shape
    gain = gain_ref[...].astype(jnp.float32)[None, :]
    for at in range(0, rows, 32):
        values = token_ref[at : at + 32, :].astype(jnp.float32)
        square = jnp.mean(values * values, axis=-1, keepdims=True)
        normed = values * lax.rsqrt(square + 1e-06) * gain
        out_ref[at : at + 32, :width] = normed.astype(jnp.bfloat16)
    logits = lax.dot_general(
        out_ref[:, :width],
        router_ref[...],
        (((1,), (1,)), ((), ())),
        preferred_element_type=jnp.float32,
    )
    routes = routes_ref[...]
    lanes = lax.broadcasted_iota(jnp.int32, (128, rows), 0)
    named = lanes == routes[0:1, :]
    for choice in range(1, routes.shape[0]):
        named = named | (lanes == routes[choice : choice + 1, :])
    named = jnp.where(named, 1.0, 0.0).T[:, :experts] > 0
    picked = jnp.where(named, jax.nn.sigmoid(logits), 0.0)
    weight = picked / jnp.sum(picked, axis=1, keepdims=True)
    weight = jnp.where(named, weight, 0.0)
    high = weight.astype(jnp.bfloat16)
    low = (weight - high.astype(jnp.float32)).astype(jnp.bfloat16)
    spare = jnp.zeros((rows, EXTRA - 2 * experts), jnp.bfloat16)
    out_ref[:, width:] = jnp.concatenate([high, low, spare], axis=1)
    for copy in copies[4:]:
        copy.wait()


def pack(gain, router, names, tokens, gate, upper):
    rows, width = tokens.shape
    depth, units = gate.shape
    small = [gain, router, names, tokens]
    return pl.pallas_call(
        functools.partial(pack_kernel, router.shape[0]),
        out_shape=(
            jax.ShapeDtypeStruct((rows, width + EXTRA), jnp.bfloat16),
            jax.ShapeDtypeStruct((2 * depth, units), jnp.bfloat16),
        ),
        in_specs=[ANYWHERE] * 6,
        out_specs=(WHOLE, WHOLE),
        scratch_shapes=[pltpu.VMEM(x.shape, x.dtype) for x in small]
        + [pltpu.SemaphoreType.DMA((6,))],
        compiler_params=params(MOST_VMEM),
        cost_estimate=cost(rows * width * 16, rows * width * 4 + 8 * depth * units),
        name="pack",
    )(*small, gate, upper)


def assemble(me, pieces, first, columns, target):
    depth = target.shape[0] // len(pieces)
    for apart, parts in enumerate(pieces):
        at = pl.multiple_of((me ^ apart) * depth, depth)
        begin = 0
        for part in parts:
            end = begin + part.shape[0]
            low, high = max(begin, first), min(end, first + depth)
            if low < high:
                place = pl.ds(pl.multiple_of(at + (low - first), 16), high - low)
                target[place, :] = part[low - begin : high - begin, columns]
            begin = end


def take_pieces(layout, refs):
    pieces, at = [], 0
    for count in layout:
        pieces.append(refs[at : at + count])
        at += count
    return pieces, refs[at:]


def stacked(pieces, first, depth):
    found = []
    for parts in pieces:
        begin = 0
        for part in parts:
            end = begin + part.shape[0]
            low, high = max(begin, first), min(end, first + depth)
            if low < high:
                found.append(part[low - begin : high - begin, :])
            begin = end
    return jnp.concatenate(found, axis=0)


def hidden_kernel(inputs, layout, me_ref, place_ref, *refs):
    blocks, refs = refs[:inputs], refs[inputs:]
    pieces, refs = take_pieces(layout, refs)
    outs, (rows_ref, gate_mat, upper_mat, sems) = refs[:-4], refs[-4:]
    width = rows_ref.shape[1] - EXTRA
    depth = width // len(pieces)
    in_place = depth % 128 == 0
    copies, at = [], 0
    for place, block in enumerate(blocks):
        target = rows_ref.at[at : at + block.shape[0], :]
        copies.append(pltpu.make_async_copy(block, target, sems.at[place]))
        copies[-1].start()
        at += block.shape[0]
    if not in_place:
        columns = slice(0, gate_mat.shape[1])
        assemble(me_ref[0], pieces, 0, columns, gate_mat)
        assemble(me_ref[0], pieces, depth, columns, upper_mat)
    lanes = lax.broadcasted_iota(jnp.int32, (1, EXTRA), 1)
    own = jnp.zeros((1, EXTRA), jnp.float32)
    experts = place_ref.shape[0]
    for expert in range(experts):
        mine = ((lanes == expert) | (lanes == expert + experts)) & (place_ref[expert] == me_ref[1])
        own = jnp.where(mine, 1.0, own)
    at, done, fetched = 0, 0, 0
    for out in outs:
        here = slice(at, at + out.shape[0])
        at += out.shape[0]
        while fetched < at:
            copies[done].wait()
            fetched += blocks[done].shape[0]
            done += 1
        weights = rows_ref[here, width:].astype(jnp.float32)
        scale = jnp.sum(weights * own, axis=1, keepdims=True)
        if in_place:
            rows = [
                rows_ref[here, pl.ds(pl.multiple_of((me_ref[0] ^ apart) * depth, depth), depth)]
                for apart in range(len(pieces))
            ]
            rows = jnp.concatenate(rows, axis=1)
            first, second = stacked(pieces, 0, depth), stacked(pieces, depth, depth)
        else:
            rows, first, second = rows_ref[here, :width], gate_mat[...], upper_mat[...]
        gate = jnp.dot(rows, first, preferred_element_type=jnp.float32)
        upper = jnp.dot(rows, second, preferred_element_type=jnp.float32)
        hidden = jnp.where(scale > 0, jnp.maximum(gate, 0.0) * upper * scale, 0.0)
        out[...] = hidden.astype(jnp.bfloat16)


def hidden_blocks(me, placement, groups, pairs):
    layout = [len(parts) for parts in pairs]
    flat = [part for parts in pairs for part in parts]
    width, units = sum(part.shape[0] for part in flat) // 2, flat[0].shape[1]
    heights = [sum(block.shape[0] for block in group) for group in groups]
    blocks = [block for group in groups for block in group]
    whole = (width, units) if width // len(pairs) % 128 else (16, 128)
    return pl.pallas_call(
        functools.partial(hidden_kernel, len(blocks), layout),
        out_shape=tuple(jax.ShapeDtypeStruct((h, units), jnp.bfloat16) for h in heights),
        in_specs=[SCALAR, SCALAR] + [ANYWHERE] * len(blocks) + [WHOLE] * len(flat),
        out_specs=tuple(WHOLE for _ in groups),
        scratch_shapes=[
            pltpu.VMEM((sum(heights), width + EXTRA), jnp.bfloat16),
            pltpu.VMEM(whole, jnp.bfloat16),
            pltpu.VMEM(whole, jnp.bfloat16),
            pltpu.SemaphoreType.DMA((len(blocks),)),
        ],
        compiler_params=params(MUCH_VMEM),
        name="hidden",
    )(me, placement, *blocks, *flat)


def down_kernel(slots, layout, column, me_ref, *refs):
    hidden, refs = refs[: len(slots)], refs[len(slots) :]
    pieces, refs = take_pieces(layout, refs)
    outs, down_mat = refs[:-1], refs[-1]
    assemble(me_ref[0], pieces, 0, slice(column, column + down_mat.shape[1]), down_mat)
    for group, parts in zip(hidden, slots):
        out = jnp.dot(group[...], down_mat[...], preferred_element_type=jnp.float32)
        at = 0
        for slot, first, count in parts:
            part = out[at : at + count, :]
            outs[slot][first : first + count, :] = part.astype(outs[slot].dtype)
            at += count


def down_blocks(me, column, width, hidden, slots, kinds, downs):
    layout = [len(parts) for parts in downs]
    pieces = [part for parts in downs for part in parts]
    units = sum(part.shape[0] for part in pieces)
    flat = [part for parts in slots for part in parts]
    heights = [sum(c for slot, _, c in flat if slot == at) for at in range(len(kinds))]
    return pl.pallas_call(
        functools.partial(down_kernel, slots, layout, column),
        out_shape=tuple(
            jax.ShapeDtypeStruct((height, width), kind) for height, kind in zip(heights, kinds)
        ),
        in_specs=[SCALAR] + [WHOLE] * (len(hidden) + len(pieces)),
        out_specs=tuple(WHOLE for _ in kinds),
        scratch_shapes=[pltpu.VMEM((units, width), jnp.bfloat16)],
        compiler_params=params(),
        name="down",
    )(me, *hidden, *pieces)


def swap_blk(value, bit):
    pairs = [(i, i ^ bit) for i in range(lax.axis_size("blk"))]
    return lax.ppermute(value, "blk", pairs)


def outer_rounds(piece):
    have = {0: piece}
    bit = lax.axis_size("blk") // 2
    while bit > 1:
        have.update({k ^ bit: swap_blk(value, bit) for k, value in list(have.items())})
        bit //= 2
    return have


def last_round(have, count, *others):
    have = {k: after(v, count, *others) if k else [v] for k, v in have.items()}
    have.update({k ^ 1: [swap_blk(part, 1) for part in parts] for k, parts in list(have.items())})
    return [have[k] for k in sorted(have)]


def add_round(*terms):
    total = terms[0].astype(jnp.float32)
    for term in terms[1:]:
        total = total + term.astype(jnp.float32)
    return total.astype(jnp.bfloat16)


def on_device(
    tokens, norm_gain, router_weight, routes, placement, gate_weight, up_weight, down_weight
):
    holders = lax.axis_size("ep")
    tok_rows, width = tokens.shape
    far = holders // 2
    order = ring_order(holders)
    ahead = [(order[i], order[(i + 1) % holders]) for i in range(holders)]
    behind = [(target, source) for source, target in ahead]

    def clock(x):
        return lax.ppermute(x, "ep", ahead)

    def counter(x):
        return lax.ppermute(x, "ep", behind)

    me = jnp.stack([lax.axis_index("blk"), lax.axis_index("ep")]).astype(jnp.int32)

    downs = outer_rounds(down_weight[0])
    packed, pair = pack(
        norm_gain, router_weight.T, routes.T, tokens, gate_weight[0], up_weight[0]
    )
    pairs = outer_rounds(pair)
    half = width // 2

    cut = tok_rows // 2
    from_behind, from_ahead = [packed], [packed]
    for step in range(1, far):
        from_ahead.append(counter(from_ahead[-1]))
        from_behind.append(clock(from_behind[-1]))
    far_parts = [clock(from_behind[-1][:cut]), counter(from_ahead[-1][cut:])]

    pairs = last_round(pairs, 4, from_behind[far - 1], from_ahead[far - 1])

    groups = [[((0, 0), 0, packed)]]
    for step in range(1, far):
        groups.append([((-1, step), 0, from_behind[step]), ((1, step), 0, from_ahead[step])])
    groups.append([((0, far), 0, far_parts[0]), ((0, far), cut, far_parts[1])])
    def only_blocks(chosen):
        return [[block for _, _, block in group] for group in chosen]

    hidden = []
    for low in range(0, len(groups), 5):
        hidden += hidden_blocks(me, placement, only_blocks(groups[low : low + 5]), pairs)
    downs = last_round(downs, 1, hidden[-1])
    results = []
    for side in range(2):
        long_way, short_way = (clock, counter) if side == 0 else (counter, clock)
        long_sign = 1 if side == 0 else -1
        sent_first = [(0, far), (-long_sign, far - 1)]
        table = {}
        cuts = [len(groups), len(groups) - 2] + list(range(len(groups) - 7, 0, -5)) + [0]
        for low, high in zip(cuts[1:], cuts):
            chosen = groups[low:high]
            keys = list(dict.fromkeys(key for group in chosen for key, _, _ in group))
            kinds = [jnp.bfloat16 if key in sent_first else jnp.float32 for key in keys]
            slots = [
                [(keys.index(key), first, block.shape[0]) for key, first, block in group]
                for group in chosen
            ]
            outs = down_blocks(me, side * half, half, hidden[low:high], slots, kinds, downs)
            table.update(zip(keys, outs))
        long_run = long_way(table[0, far])
        short_run = short_way(table[-long_sign, far - 1])
        for step in range(far - 1, 0, -1):
            long_run = long_way(add_round(long_run, table[long_sign, step]))
            if step > 1:
                short_run = short_way(add_round(short_run, table[-long_sign, step - 1]))
        results.append(add_round(table[0, 0], long_run, short_run))
    return jnp.concatenate(results, axis=1)


def solution(mesh):
    in_specs = (
        P(("ep", "blk"), None),
        P(),
        P(),
        P(("ep", "blk"), None),
        P(),
        P("ep", "blk", None),
        P("ep", "blk", None),
        P("ep", "blk", None),
    )
    out_specs = P(("ep", "blk"), None)
    return jax.shard_map(
        on_device, mesh=mesh, in_specs=in_specs, out_specs=out_specs, check_vma=False
    )
```

```python
import functools

import jax
import jax.numpy as jnp
from jax import lax
from jax.experimental import pallas as pl
from jax.experimental.pallas import tpu as pltpu
from jax.sharding import PartitionSpec as P

VMEM_LIMIT = 28 * 1024 * 1024
MOST_VMEM = 60 * 1024 * 1024
MUCH_VMEM = 52 * 1024 * 1024
EXTRA = 128
WHOLE = pl.BlockSpec(memory_space=pltpu.VMEM)
SCALAR = pl.BlockSpec(memory_space=pltpu.SMEM)
ANYWHERE = pl.BlockSpec(memory_space=pl.ANY)


def params(limit=VMEM_LIMIT):
    return pltpu.CompilerParams(vmem_limit_bytes=limit)


def cost(flops, moved):
    return pl.CostEstimate(flops=int(flops), bytes_accessed=int(moved), transcendentals=0)


def ring_order(holders):
    columns = 1
    while 2 * (columns * 2) ** 2 <= holders:
        columns *= 2
    columns = max(columns, 2) if holders >= 4 else 1
    rows = holders // columns
    order = [row * columns for row in range(rows)]
    for back, row in enumerate(reversed(range(rows))):
        line = range(1, columns) if back % 2 == 0 else reversed(range(1, columns))
        order += [row * columns + column for column in line]
    return order


def after_kernel(count, value_ref, *refs):
    outs = refs[len(refs) - count :]
    rows = outs[0].shape[0]
    for at, out in enumerate(outs):
        out[...] = value_ref[at * rows : (at + 1) * rows, :]


def after(value, count, *others):
    marks = [other[:8, :128] for other in others]
    part = jax.ShapeDtypeStruct((value.shape[0] // count, value.shape[1]), value.dtype)
    return pl.pallas_call(
        functools.partial(after_kernel, count),
        out_shape=(part,) * count,
        in_specs=[WHOLE] * (1 + len(marks)),
        out_specs=(WHOLE,) * count,
        compiler_params=params(),
        name="after",
    )(value, *marks)


def pack_kernel(experts, *refs):
    sources, (out_ref, pair_ref, gain_ref, router_ref, routes_ref, token_ref, sems) = refs[:6], refs[6:]
    depth = sources[4].shape[0]
    targets = [gain_ref, router_ref, routes_ref, token_ref]
    targets += [pair_ref.at[:depth, :], pair_ref.at[depth:, :]]
    copies = [
        pltpu.make_async_copy(source, target, sems.at[at])
        for at, (source, target) in enumerate(zip(sources, targets))
    ]
    for copy in copies:
        copy.start()
    for copy in copies[:4]:
        copy.wait()
    rows, width = token_ref.shape
    gain = gain_ref[...].astype(jnp.float32)[None, :]
    for at in range(0, rows, 32):
        values = token_ref[at : at + 32, :].astype(jnp.float32)
        square = jnp.mean(values * values, axis=-1, keepdims=True)
        normed = values * lax.rsqrt(square + 1e-06) * gain
        out_ref[at : at + 32, :width] = normed.astype(jnp.bfloat16)
    logits = lax.dot_general(
        out_ref[:, :width],
        router_ref[...],
        (((1,), (1,)), ((), ())),
        preferred_element_type=jnp.float32,
    )
    routes = routes_ref[...]
    lanes = lax.broadcasted_iota(jnp.int32, (128, rows), 0)
    named = lanes == routes[0:1, :]
    for choice in range(1, routes.shape[0]):
        named = named | (lanes == routes[choice : choice + 1, :])
    named = jnp.where(named, 1.0, 0.0).T[:, :experts] > 0
    picked = jnp.where(named, jax.nn.sigmoid(logits), 0.0)
    weight = picked / jnp.sum(picked, axis=1, keepdims=True)
    weight = jnp.where(named, weight, 0.0)
    high = weight.astype(jnp.bfloat16)
    low = (weight - high.astype(jnp.float32)).astype(jnp.bfloat16)
    spare = jnp.zeros((rows, EXTRA - 2 * experts), jnp.bfloat16)
    out_ref[:, width:] = jnp.concatenate([high, low, spare], axis=1)
    for copy in copies[4:]:
        copy.wait()


def pack(gain, router, names, tokens, gate, upper):
    rows, width = tokens.shape
    depth, units = gate.shape
    small = [gain, router, names, tokens]
    return pl.pallas_call(
        functools.partial(pack_kernel, router.shape[0]),
        out_shape=(
            jax.ShapeDtypeStruct((rows, width + EXTRA), jnp.bfloat16),
            jax.ShapeDtypeStruct((2 * depth, units), jnp.bfloat16),
        ),
        in_specs=[ANYWHERE] * 6,
        out_specs=(WHOLE, WHOLE),
        scratch_shapes=[pltpu.VMEM(x.shape, x.dtype) for x in small]
        + [pltpu.SemaphoreType.DMA((6,))],
        compiler_params=params(MOST_VMEM),
        cost_estimate=cost(rows * width * 16, rows * width * 4 + 8 * depth * units),
        name="pack",
    )(*small, gate, upper)


def assemble(me, pieces, first, columns, target):
    depth = target.shape[0] // len(pieces)
    for apart, parts in enumerate(pieces):
        at = pl.multiple_of((me ^ apart) * depth, depth)
        begin = 0
        for part in parts:
            end = begin + part.shape[0]
            low, high = max(begin, first), min(end, first + depth)
            if low < high:
                place = pl.ds(pl.multiple_of(at + (low - first), 16), high - low)
                target[place, :] = part[low - begin : high - begin, columns]
            begin = end


def take_pieces(layout, refs):
    pieces, at = [], 0
    for count in layout:
        pieces.append(refs[at : at + count])
        at += count
    return pieces, refs[at:]


def stacked(pieces, first, depth):
    found = []
    for parts in pieces:
        begin = 0
        for part in parts:
            end = begin + part.shape[0]
            low, high = max(begin, first), min(end, first + depth)
            if low < high:
                found.append(part[low - begin : high - begin, :])
            begin = end
    return jnp.concatenate(found, axis=0)


def hidden_kernel(inputs, layout, me_ref, place_ref, *refs):
    blocks, refs = refs[:inputs], refs[inputs:]
    pieces, refs = take_pieces(layout, refs)
    outs, (rows_ref, gate_mat, upper_mat, sems) = refs[:-4], refs[-4:]
    width = rows_ref.shape[1] - EXTRA
    depth = width // len(pieces)
    in_place = depth % 128 == 0
    copies, at = [], 0
    for place, block in enumerate(blocks):
        target = rows_ref.at[at : at + block.shape[0], :]
        copies.append(pltpu.make_async_copy(block, target, sems.at[place]))
        copies[-1].start()
        at += block.shape[0]
    if not in_place:
        columns = slice(0, gate_mat.shape[1])
        assemble(me_ref[0], pieces, 0, columns, gate_mat)
        assemble(me_ref[0], pieces, depth, columns, upper_mat)
    lanes = lax.broadcasted_iota(jnp.int32, (1, EXTRA), 1)
    own = jnp.zeros((1, EXTRA), jnp.float32)
    experts = place_ref.shape[0]
    for expert in range(experts):
        mine = ((lanes == expert) | (lanes == expert + experts)) & (place_ref[expert] == me_ref[1])
        own = jnp.where(mine, 1.0, own)
    at, done, fetched = 0, 0, 0
    for out in outs:
        here = slice(at, at + out.shape[0])
        at += out.shape[0]
        while fetched < at:
            copies[done].wait()
            fetched += blocks[done].shape[0]
            done += 1
        weights = rows_ref[here, width:].astype(jnp.float32)
        scale = jnp.sum(weights * own, axis=1, keepdims=True)
        if in_place:
            rows = [
                rows_ref[here, pl.ds(pl.multiple_of((me_ref[0] ^ apart) * depth, depth), depth)]
                for apart in range(len(pieces))
            ]
            rows = jnp.concatenate(rows, axis=1)
            first, second = stacked(pieces, 0, depth), stacked(pieces, depth, depth)
        else:
            rows, first, second = rows_ref[here, :width], gate_mat[...], upper_mat[...]
        gate = jnp.dot(rows, first, preferred_element_type=jnp.float32)
        upper = jnp.dot(rows, second, preferred_element_type=jnp.float32)
        hidden = jnp.where(scale > 0, jnp.maximum(gate, 0.0) * upper * scale, 0.0)
        out[...] = hidden.astype(jnp.bfloat16)


def hidden_blocks(me, placement, groups, pairs):
    layout = [len(parts) for parts in pairs]
    flat = [part for parts in pairs for part in parts]
    width, units = sum(part.shape[0] for part in flat) // 2, flat[0].shape[1]
    heights = [sum(block.shape[0] for block in group) for group in groups]
    blocks = [block for group in groups for block in group]
    whole = (width, units) if width // len(pairs) % 128 else (16, 128)
    return pl.pallas_call(
        functools.partial(hidden_kernel, len(blocks), layout),
        out_shape=tuple(jax.ShapeDtypeStruct((h, units), jnp.bfloat16) for h in heights),
        in_specs=[SCALAR, SCALAR] + [ANYWHERE] * len(blocks) + [WHOLE] * len(flat),
        out_specs=tuple(WHOLE for _ in groups),
        scratch_shapes=[
            pltpu.VMEM((sum(heights), width + EXTRA), jnp.bfloat16),
            pltpu.VMEM(whole, jnp.bfloat16),
            pltpu.VMEM(whole, jnp.bfloat16),
            pltpu.SemaphoreType.DMA((len(blocks),)),
        ],
        compiler_params=params(MUCH_VMEM),
        name="hidden",
    )(me, placement, *blocks, *flat)


def down_kernel(slots, layout, column, me_ref, *refs):
    hidden, refs = refs[: len(slots)], refs[len(slots) :]
    pieces, refs = take_pieces(layout, refs)
    outs, down_mat = refs[:-1], refs[-1]
    assemble(me_ref[0], pieces, 0, slice(column, column + down_mat.shape[1]), down_mat)
    for group, parts in zip(hidden, slots):
        out = jnp.dot(group[...], down_mat[...], preferred_element_type=jnp.float32)
        at = 0
        for slot, first, count in parts:
            part = out[at : at + count, :]
            outs[slot][first : first + count, :] = part.astype(outs[slot].dtype)
            at += count


def down_blocks(me, column, width, hidden, slots, kinds, downs):
    layout = [len(parts) for parts in downs]
    pieces = [part for parts in downs for part in parts]
    units = sum(part.shape[0] for part in pieces)
    flat = [part for parts in slots for part in parts]
    heights = [sum(c for slot, _, c in flat if slot == at) for at in range(len(kinds))]
    return pl.pallas_call(
        functools.partial(down_kernel, slots, layout, column),
        out_shape=tuple(
            jax.ShapeDtypeStruct((height, width), kind) for height, kind in zip(heights, kinds)
        ),
        in_specs=[SCALAR] + [WHOLE] * (len(hidden) + len(pieces)),
        out_specs=tuple(WHOLE for _ in kinds),
        scratch_shapes=[pltpu.VMEM((units, width), jnp.bfloat16)],
        compiler_params=params(),
        name="down",
    )(me, *hidden, *pieces)


def swap_blk(value, bit):
    pairs = [(i, i ^ bit) for i in range(lax.axis_size("blk"))]
    return lax.ppermute(value, "blk", pairs)


def outer_rounds(piece):
    have = {0: piece}
    bit = lax.axis_size("blk") // 2
    while bit > 1:
        have.update({k ^ bit: swap_blk(value, bit) for k, value in list(have.items())})
        bit //= 2
    return have


def last_round(have, count, *others):
    have = {k: after(v, count, *others) if k else [v] for k, v in have.items()}
    have.update({k ^ 1: [swap_blk(part, 1) for part in parts] for k, parts in list(have.items())})
    return [have[k] for k in sorted(have)]


def add_round(*terms):
    total = terms[0].astype(jnp.float32)
    for term in terms[1:]:
        total = total + term.astype(jnp.float32)
    return total.astype(jnp.bfloat16)


def finish_kernel(*refs):
    out_ref, width = refs[-1], refs[0].shape[1]
    for side in range(2):
        total = refs[3 * side][...].astype(jnp.float32)
        for ref in refs[3 * side + 1 : 3 * side + 3]:
            total = total + ref[...].astype(jnp.float32)
        out_ref[:, side * width : (side + 1) * width] = total.astype(jnp.bfloat16)


def finish(terms):
    rows, width = terms[0].shape
    return pl.pallas_call(
        finish_kernel,
        out_shape=jax.ShapeDtypeStruct((rows, 2 * width), jnp.bfloat16),
        in_specs=[WHOLE] * len(terms),
        out_specs=WHOLE,
        compiler_params=params(),
        name="finish",
    )(*terms)


def on_device(
    tokens, norm_gain, router_weight, routes, placement, gate_weight, up_weight, down_weight
):
    holders = lax.axis_size("ep")
    tok_rows, width = tokens.shape
    far = holders // 2
    order = ring_order(holders)
    ahead = [(order[i], order[(i + 1) % holders]) for i in range(holders)]
    behind = [(target, source) for source, target in ahead]

    def clock(x):
        return lax.ppermute(x, "ep", ahead)

    def counter(x):
        return lax.ppermute(x, "ep", behind)

    me = jnp.stack([lax.axis_index("blk"), lax.axis_index("ep")]).astype(jnp.int32)

    downs = outer_rounds(down_weight[0])
    packed, pair = pack(
        norm_gain, router_weight.T, routes.T, tokens, gate_weight[0], up_weight[0]
    )
    pairs = outer_rounds(pair)
    half = width // 2

    cut = tok_rows // 2
    from_behind, from_ahead = [packed], [packed]
    for step in range(1, far):
        from_ahead.append(counter(from_ahead[-1]))
        from_behind.append(clock(from_behind[-1]))
    far_parts = [clock(from_behind[-1][:cut]), counter(from_ahead[-1][cut:])]

    pairs = last_round(pairs, 4, from_behind[far - 1], from_ahead[far - 1])

    groups = [[((0, 0), 0, packed)]]
    for step in range(1, far):
        groups.append([((-1, step), 0, from_behind[step]), ((1, step), 0, from_ahead[step])])
    groups.append([((0, far), 0, far_parts[0]), ((0, far), cut, far_parts[1])])
    def only_blocks(chosen):
        return [[block for _, _, block in group] for group in chosen]

    hidden = []
    for low in range(0, len(groups), 5):
        hidden += hidden_blocks(me, placement, only_blocks(groups[low : low + 5]), pairs)
    downs = last_round(downs, 1, hidden[-1])
    results = []
    for side in range(2):
        long_way, short_way = (clock, counter) if side == 0 else (counter, clock)
        long_sign = 1 if side == 0 else -1
        sent_first = [(0, far), (-long_sign, far - 1)]
        table = {}
        cuts = [len(groups), len(groups) - 2] + list(range(len(groups) - 7, 0, -5)) + [0]
        for low, high in zip(cuts[1:], cuts):
            chosen = groups[low:high]
            keys = list(dict.fromkeys(key for group in chosen for key, _, _ in group))
            kinds = [jnp.bfloat16 if key in sent_first else jnp.float32 for key in keys]
            slots = [
                [(keys.index(key), first, block.shape[0]) for key, first, block in group]
                for group in chosen
            ]
            outs = down_blocks(me, side * half, half, hidden[low:high], slots, kinds, downs)
            table.update(zip(keys, outs))
        long_run = long_way(table[0, far])
        short_run = short_way(table[-long_sign, far - 1])
        for step in range(far - 1, 0, -1):
            long_run = long_way(add_round(long_run, table[long_sign, step]))
            if step > 1:
                short_run = short_way(add_round(short_run, table[-long_sign, step - 1]))
        results += [table[0, 0], long_run, short_run]
    return finish(results)


def solution(mesh):
    in_specs = (
        P(("ep", "blk"), None),
        P(),
        P(),
        P(("ep", "blk"), None),
        P(),
        P("ep", "blk", None),
        P("ep", "blk", None),
        P("ep", "blk", None),
    )
    out_specs = P(("ep", "blk"), None)
    return jax.shard_map(
        on_device, mesh=mesh, in_specs=in_specs, out_specs=out_specs, check_vma=False
    )
```
